32 devices in a mesh: groups: 2 (over y), res: 16 (over z, x, core), feat: 1.
Axes of the slice: x: 2, y: 2, z: 4, core: 2. Of those that a mesh axis runs over, the one named last changes fastest.
Arguments:
- node_feats: bfloat16 [2048, 512], P(('groups', 'res')), parts along dimension 0, may hold values from -6 to 6
- edge_feats: bfloat16 [2048, 20, 256], P(('groups', 'res')), parts along dimension 0, may hold values from -6 to 6
- neighbours: int32 [2048, 20], P(('groups', 'res')), parts along dimension 0, may hold values from 0 to 1023, as said below
- w_self: bfloat16 [512, 256], P(None, 'feat'), may hold values from -0.25 to 0.25
- w_nbr: bfloat16 [512, 256], P(None, 'feat'), may hold values from -0.25 to 0.25
- w_edge: bfloat16 [256, 256], P(None, 'feat'), may hold values from -0.375 to 0.375
- bias: float32 [256], P('feat'), may hold values from -3 to 3
- w_edge_out: bfloat16 [256, 256], P('feat'), may hold values from -0.375 to 0.375
- w_node_out: bfloat16 [256, 512], P('feat'), may hold values from -0.375 to 0.375
- grad_nodes: bfloat16 [2048, 512], P(('groups', 'res')), parts along dimension 0, may hold values from -6 to 6
- grad_edges: bfloat16 [2048, 20, 256], P(('groups', 'res')), parts along dimension 0, may hold values from -6 to 6
Outputs:
- d_nodes: bfloat16 [2048, 512], P(('groups', 'res'), 'feat'), parts along dimension 0
- d_edges: bfloat16 [2048, 20, 256], P(('groups', 'res'), None, 'feat'), parts along dimension 0
- d_self: bfloat16 [1024, 256], P('groups', 'feat'), parts along dimension 0
- d_nbr: bfloat16 [1024, 256], P('groups', 'feat'), parts along dimension 0
- d_edge_in: bfloat16 [512, 256], P('groups', 'feat'), parts along dimension 0
- d_bias: float32 [512], P(('groups', 'feat')), parts along dimension 0
- d_edge_out: bfloat16 [512, 256], P(('groups', 'feat')), parts along dimension 0
- d_node_out: bfloat16 [512, 512], P(('groups', 'feat')), parts along dimension 0
The draws below stay inside these ranges and needn't reach their ends.
There are 2 independent parts, one for each index of `groups`. The reference program is written for one: setup_inputs(seed, part) draws one part's arguments, and reference() takes and returns one part's arrays. A program takes and returns all parts, laid end to end along the dimension named above; an argument that names none is the same for every part. Nothing has to cross between parts.
Inputs may be any that keep to these rules, and one draw needn't show every extreme that they name: For k < 12, neighbours[i,k] differs from i by 1 to 64. For k >= 12: in each aligned block of 64 rows, at most 33 of these entries fall into any one aligned block of 64 residues, and exactly 33 into some block.
All inputs are finite; a program needn't handle non-finite values.
Results may differ from the reference program's by a relative error of at most 0.014.
Values may be sent and summed in bfloat16 or wider, within the bound.
A program may use at most 64 MiB of HBM per device.

```python
import jax
import jax.numpy as jnp
from jax import lax

DN = 512
DE = 256
HID = 256
RES_DEV = 64
KL = 12
KR = 8
K = 20
CAP = 33
NODES = 1024
N_RES = 16


def draw_neighbours(key, part):
    key = jax.random.fold_in(key, 7)
    key_offset, key_sign, key_long = jax.random.split(key, 3)
    nodes_all = RES_DEV * N_RES
    row_ids = jnp.arange(nodes_all, dtype=jnp.int32)[:, None]
    offsets = jax.random.randint(key_offset, (nodes_all, KL), 1, RES_DEV + 1)
    signs = jax.random.randint(key_sign, (nodes_all, KL), 0, 2) * 2 - 1
    target = row_ids + offsets * signs
    outside = (target < 0) | (target >= nodes_all)
    target = jnp.where(outside, row_ids - offsets * signs, target)
    total_slots = N_RES * CAP
    picked = RES_DEV * KR

    def one_block(block_key):
        key_order, key_mix, key_rows = jax.random.split(block_key, 3)
        order = jax.random.permutation(key_order, total_slots)
        positions = jnp.argsort(order)
        full_peer = order[0] // CAP
        slot_ids = jnp.arange(total_slots, dtype=jnp.int32)
        priority = jnp.where(slot_ids // CAP == full_peer, -1, positions)
        chosen = jnp.argsort(priority, stable=True)[:picked]
        chosen = jax.random.permutation(key_mix, chosen)
        inner_rows = jax.random.randint(key_rows, (picked,), 0, RES_DEV)
        return (chosen // CAP * RES_DEV + inner_rows).reshape(RES_DEV, KR)
    longs = jax.vmap(one_block)(jax.random.split(key_long, N_RES)).reshape(nodes_all, KR)
    return jnp.concatenate([target, longs], axis=1).astype(jnp.int32)


def block_scale(own_key, extent, pieces, smallest, top_value):
    factor_of = 1.0
    for dim, parts in pieces:
        heights = jax.random.uniform(jax.random.fold_in(jax.random.fold_in(own_key, 6), dim), (parts,), jnp.float32, smallest / len(pieces), top_value / len(pieces))
        factor_of = factor_of * jnp.repeat(jnp.exp(heights), extent[dim] // parts).reshape((-1,) + (1,) * (len(extent) - 1 - dim))
    return factor_of


def noise(rng, shape, spread, limit, cuts=(), kind=jnp.bfloat16):
    values = spread * jax.random.normal(rng, shape, jnp.float32)
    if cuts:
        values = values * block_scale(rng, shape, cuts, -0.22, 0.18)
    return jnp.clip(values, -limit, limit).astype(kind)


def setup_inputs(seed: int = 0, part: int = 0) -> dict:
    splits = jax.random.split(jax.random.key(seed), 12)
    part_splits = jax.random.split(jax.random.fold_in(splits[11], part), 12)
    return {
        "node_feats": noise(part_splits[0], (NODES, DN), 1.0, 6.0, ((0, 16),)),
        "edge_feats": noise(part_splits[1], (NODES, K, DE), 1.0, 6.0, ((0, 16),)),
        "neighbours": draw_neighbours(jax.random.fold_in(jax.random.fold_in(splits[11], part), 71), part),
        "w_self": noise(splits[3], (DN, HID), DN ** -0.5, 0.25),
        "w_nbr": noise(splits[4], (DN, HID), DN ** -0.5, 0.25),
        "w_edge": noise(splits[5], (DE, HID), DE ** -0.5, 0.375),
        "bias": noise(splits[6], (HID,), 0.5, 3.0, (), jnp.float32),
        "w_edge_out": noise(splits[7], (HID, DE), HID ** -0.5, 0.375),
        "w_node_out": noise(splits[8], (HID, DN), HID ** -0.5, 0.375),
        "grad_nodes": noise(part_splits[9], (NODES, DN), 1.0, 6.0, ((0, 16),)),
        "grad_edges": noise(part_splits[10], (NODES, K, DE), 1.0, 6.0, ((0, 16),)),
    }


gelu_scale = 0.7978845608028654
gelu_cubic = 0.044715


def gelu_parts(preact):
    inner = gelu_scale * (preact + gelu_cubic * preact * preact * preact)
    tangent = jnp.tanh(inner)
    values = 0.5 * preact * (1.0 + tangent)
    slopes = 0.5 * (1.0 + tangent) + 0.5 * preact * (1.0 - tangent * tangent) * gelu_scale * (1.0 + 3.0 * gelu_cubic * preact * preact)
    return values, slopes


def contract_rows(left, right):
    return lax.dot_general(left, right, (((0,), (0,)), ((), ())), preferred_element_type=jnp.float32)


def reference(node_feats, edge_feats, neighbours, w_self, w_nbr, w_edge, bias, w_edge_out, w_node_out, grad_nodes, grad_edges):
    nodes_all = node_feats.shape[0]
    blocks = nodes_all // RES_DEV
    edges_blk = RES_DEV * K
    hidden = w_self.shape[1]

    def one_block(carry, block_index):
        acc_self, acc_nbr, acc_edge, acc_bias, acc_eout, acc_nout, node_acc = carry
        first_row = block_index * RES_DEV
        own_rows = lax.dynamic_slice_in_dim(node_feats, first_row, RES_DEV, 0)
        own_edges = lax.dynamic_slice_in_dim(edge_feats, first_row, RES_DEV, 0).reshape(edges_blk, DE)
        own_nbrs = lax.dynamic_slice_in_dim(neighbours, first_row, RES_DEV, 0).reshape(-1).astype(jnp.int32)
        own_gnode = lax.dynamic_slice_in_dim(grad_nodes, first_row, RES_DEV, 0)
        own_gedge = lax.dynamic_slice_in_dim(grad_edges, first_row, RES_DEV, 0).reshape(edges_blk, DE)
        nbr_rows = jnp.take(node_feats, own_nbrs, axis=0)
        preact = jnp.dot(own_rows, w_self, preferred_element_type=jnp.float32)[:, None, :]
        preact = preact + jnp.dot(nbr_rows, w_nbr, preferred_element_type=jnp.float32).reshape(RES_DEV, K, hidden)
        preact = preact + jnp.dot(own_edges, w_edge, preferred_element_type=jnp.float32).reshape(RES_DEV, K, hidden)
        preact = preact + bias
        values, slopes = gelu_parts(preact)
        message = values.astype(jnp.bfloat16)
        grad_msg = jnp.dot(own_gedge, w_edge_out.T, preferred_element_type=jnp.float32).reshape(RES_DEV, K, hidden)
        grad_msg = grad_msg + (jnp.dot(own_gnode, w_node_out.T, preferred_element_type=jnp.float32) / K)[:, None, :]
        grad_pre = (grad_msg * slopes).astype(jnp.bfloat16)
        pre_flat = grad_pre.reshape(edges_blk, hidden)
        msg_flat = message.reshape(edges_blk, hidden)
        pre_sum = jnp.sum(grad_pre.astype(jnp.float32), axis=1).astype(jnp.bfloat16)
        msg_sum = jnp.sum(message.astype(jnp.float32), axis=1).astype(jnp.bfloat16)
        acc_self = acc_self + contract_rows(own_rows, pre_sum)
        acc_nbr = acc_nbr + contract_rows(nbr_rows, pre_flat)
        acc_edge = acc_edge + contract_rows(own_edges, pre_flat)
        acc_bias = acc_bias + jnp.sum(pre_flat.astype(jnp.float32), axis=0)
        acc_eout = acc_eout + contract_rows(msg_flat, own_gedge)
        acc_nout = acc_nout + contract_rows(msg_sum, own_gnode) / K
        edge_grad = (jnp.dot(pre_flat, w_edge.T, preferred_element_type=jnp.float32) + own_gedge.astype(jnp.float32)).astype(jnp.bfloat16)
        row_ids = first_row + jnp.arange(RES_DEV, dtype=jnp.int32)
        node_acc = node_acc.at[row_ids].add(jnp.dot(pre_sum, w_self.T, preferred_element_type=jnp.float32))
        node_acc = node_acc.at[own_nbrs].add(jnp.dot(pre_flat, w_nbr.T, preferred_element_type=jnp.float32))
        return (acc_self, acc_nbr, acc_edge, acc_bias, acc_eout, acc_nout, node_acc), edge_grad.reshape(RES_DEV, K, DE)

    start_carry = (jnp.zeros((DN, hidden), jnp.float32), jnp.zeros((DN, hidden), jnp.float32), jnp.zeros((DE, hidden), jnp.float32), jnp.zeros((hidden,), jnp.float32), jnp.zeros((hidden, DE), jnp.float32), jnp.zeros((hidden, DN), jnp.float32), jnp.zeros((nodes_all, DN), jnp.float32))
    final_carry, edge_grads = lax.scan(one_block, start_carry, jnp.arange(blocks, dtype=jnp.int32))
    acc_self, acc_nbr, acc_edge, acc_bias, acc_eout, acc_nout, node_acc = final_carry
    d_nodes = (node_acc + grad_nodes.astype(jnp.float32)).astype(jnp.bfloat16)
    d_edges = edge_grads.reshape(nodes_all, K, DE)
    return (d_nodes, d_edges, acc_self.astype(jnp.bfloat16), acc_nbr.astype(jnp.bfloat16), acc_edge.astype(jnp.bfloat16), acc_bias, acc_eout.astype(jnp.bfloat16), acc_nout.astype(jnp.bfloat16))
```

```python
import jax
import jax.numpy as jnp
from jax import lax
from jax.sharding import PartitionSpec as P

gelu_scale = 0.7978845608028654
gelu_cubic = 0.044715


def gelu_parts(preact):
    inner = gelu_scale * (preact + gelu_cubic * preact * preact * preact)
    tangent = jnp.tanh(inner)
    values = 0.5 * preact * (1.0 + tangent)
    slopes = 0.5 * (1.0 + tangent) + 0.5 * preact * (1.0 - tangent * tangent) * gelu_scale * (
        1.0 + 3.0 * gelu_cubic * preact * preact
    )
    return (values, slopes)


def contract_rows(left, right):
    return lax.dot_general(
        left, right, (((0,), (0,)), ((), ())), preferred_element_type=jnp.float32
    )


def local(
    node_feats,
    edge_feats,
    neighbours,
    w_self,
    w_nbr,
    w_edge,
    bias,
    w_edge_out,
    w_node_out,
    grad_nodes,
    grad_edges,
):
    res_rows = node_feats.shape[0]
    nbr_count = neighbours.shape[1]
    node_width = node_feats.shape[1]
    edge_width = edge_feats.shape[2]
    hidden = w_self.shape[1]
    edges_dev = res_rows * nbr_count
    blocks_res = lax.axis_size("res")
    nodes_all = res_rows * blocks_res
    edge_flat = edge_feats.reshape(edges_dev, edge_width)
    gedge_flat = grad_edges.reshape(edges_dev, edge_width)
    projected = jnp.dot(node_feats, w_nbr, preferred_element_type=jnp.float32).astype(jnp.bfloat16)
    table = lax.all_gather(projected, "res", axis=0, tiled=True)
    picks = (
        neighbours.reshape(-1)[:, None] == jnp.arange(nodes_all, dtype=jnp.int32)[None, :]
    ).astype(jnp.bfloat16)
    preact = (jnp.dot(node_feats, w_self, preferred_element_type=jnp.float32) + bias)[:, None, :]
    preact = preact + (
        jnp.dot(edge_flat, w_edge, preferred_element_type=jnp.float32)
        + jnp.dot(picks, table, preferred_element_type=jnp.float32)
    ).reshape(res_rows, nbr_count, hidden)
    values, slopes = gelu_parts(preact)
    message = values.astype(jnp.bfloat16)
    grad_msg = jnp.dot(gedge_flat, w_edge_out.T, preferred_element_type=jnp.float32).reshape(
        res_rows, nbr_count, hidden
    )
    grad_msg = (
        grad_msg
        + (jnp.dot(grad_nodes, w_node_out.T, preferred_element_type=jnp.float32) / nbr_count)[
            :, None, :
        ]
    )
    grad_pre = (grad_msg * slopes).astype(jnp.bfloat16)
    pre_flat = grad_pre.reshape(edges_dev, hidden)
    msg_flat = message.reshape(edges_dev, hidden)
    pre_sum = jnp.sum(grad_pre.astype(jnp.float32), axis=1).astype(jnp.bfloat16)
    msg_sum = jnp.sum(message.astype(jnp.float32), axis=1).astype(jnp.bfloat16)
    spread = contract_rows(picks, pre_flat).astype(jnp.bfloat16)
    landed = lax.all_to_all(
        spread.reshape(blocks_res, res_rows, hidden), "res", split_axis=0, concat_axis=0, tiled=True
    )
    reached = jnp.sum(landed.astype(jnp.float32), axis=0).astype(jnp.bfloat16)
    terms = (
        contract_rows(node_feats, pre_sum),
        contract_rows(node_feats, reached),
        contract_rows(edge_flat, pre_flat),
        contract_rows(msg_flat, gedge_flat),
        contract_rows(msg_sum, grad_nodes) / nbr_count,
    )
    packed = jnp.concatenate(
        [t.astype(jnp.bfloat16).reshape(blocks_res, -1, 128) for t in terms], axis=1
    )
    swapped = lax.all_to_all(packed, "res", split_axis=0, concat_axis=0, tiled=True)
    mine = jnp.sum(swapped.astype(jnp.float32), axis=0).astype(jnp.bfloat16)
    totals = lax.all_gather(mine, "res", axis=0, tiled=False)
    outs = []
    start = 0
    for t in terms:
        rows = t.size // blocks_res // 128
        outs.append(totals[:, start : start + rows].reshape(t.shape))
        start += rows
    grad_self, grad_nbr, grad_edge_in, grad_eout, grad_nout = outs
    grad_bias = lax.psum(jnp.sum(pre_flat.astype(jnp.float32), axis=0), "res")
    feat_index = lax.axis_index("feat")
    feat_count = lax.axis_size("feat")
    edge_part = edge_width // feat_count
    node_part = node_width // feat_count
    full_pre, full_wedge = (
        lax.all_gather(pre_flat, "feat", axis=1, tiled=True),
        lax.all_gather(w_edge, "feat", axis=1, tiled=True),
    )
    own_wedge = lax.dynamic_slice_in_dim(full_wedge, feat_index * edge_part, edge_part, 0)
    edge_summed = jnp.dot(full_pre, own_wedge.T, preferred_element_type=jnp.float32)
    gedge_part = lax.dynamic_slice_in_dim(gedge_flat, feat_index * edge_part, edge_part, 1).astype(
        jnp.float32
    )
    d_edges = (
        (edge_summed + gedge_part).astype(jnp.bfloat16).reshape(res_rows, nbr_count, edge_part)
    )
    node_total = jnp.dot(pre_sum, w_self.T, preferred_element_type=jnp.float32) + jnp.dot(
        reached, w_nbr.T, preferred_element_type=jnp.float32
    )
    node_total = lax.psum_scatter(node_total, "feat", scatter_dimension=1, tiled=True)
    gnode_part = lax.dynamic_slice_in_dim(grad_nodes, feat_index * node_part, node_part, 1).astype(
        jnp.float32
    )
    d_nodes = (node_total + gnode_part).astype(jnp.bfloat16)
    return (d_nodes, d_edges, grad_self, grad_nbr, grad_edge_in, grad_bias, grad_eout, grad_nout)


def solution(mesh):
    in_specs = (
        P(("groups", "res"), None),
        P(("groups", "res"), None, None),
        P(("groups", "res"), None),
        P(None, "feat"),
        P(None, "feat"),
        P(None, "feat"),
        P("feat"),
        P("feat", None),
        P("feat", None),
        P(("groups", "res"), None),
        P(("groups", "res"), None, None),
    )
    out_specs = (
        P(("groups", "res"), "feat"),
        P(("groups", "res"), None, "feat"),
        P("groups", "feat"),
        P("groups", "feat"),
        P("groups", "feat"),
        P(("groups", "feat")),
        P(("groups", "feat"), None),
        P(("groups", "feat"), None),
    )
    return jax.shard_map(local, mesh=mesh, in_specs=in_specs, out_specs=out_specs, check_vma=False)
```

```python
import functools

import jax
import jax.numpy as jnp
from jax import lax
from jax.experimental import pallas as pl
from jax.experimental.pallas import tpu as pltpu
from jax.sharding import PartitionSpec as P

gelu_scale = 0.7978845608028654
gelu_cubic = 0.044715


def gelu_parts(preact):
    inner = gelu_scale * (preact + gelu_cubic * preact * preact * preact)
    tangent = jnp.tanh(inner)
    values = 0.5 * preact * (1.0 + tangent)
    slopes = 0.5 * (1.0 + tangent) + 0.5 * preact * (1.0 - tangent * tangent) * gelu_scale * (
        1.0 + 3.0 * gelu_cubic * preact * preact
    )
    return (values, slopes)


def contract_rows(left, right):
    return lax.dot_general(
        left, right, (((0,), (0,)), ((), ())), preferred_element_type=jnp.float32
    )


def exchange_kernel(
    axis_count,
    nbr_count,
    node_ref,
    edge_ref,
    nbr_col_ref,
    nbr_row_ref,
    wself_ref,
    wnbr_ref,
    wedge_ref,
    bias_ref,
    weout_ref,
    wnout_ref,
    gnode_ref,
    gedge_ref,
    dnode_ref,
    dedge_ref,
    dself_ref,
    dnbr_ref,
    dein_ref,
    dbias_ref,
    deout_ref,
    dnout_ref,
    table,
    picks,
    picks_t,
    base_pre,
    base_msg,
    pre_buf,
    msg_buf,
    self_rep,
    out_rep,
    s_buf,
    s_mid,
    s_own,
    s_in,
    w_buf,
    w_mid,
    w_own,
    w_in,
    n_buf,
    n_mid,
    n_own,
    n_in,
    w_all,
    n_all,
    pair_send,
    pair_recv,
    chip_send,
    chip_recv,
    all_send,
    all_recv,
):
    f32, bf16 = jnp.float32, jnp.bfloat16
    chips = axis_count // 2
    me = lax.axis_index("res")
    core = lax.rem(me, 2)
    chip = lax.div(me, 2)
    sibling = me + 1 - 2 * core
    rows, width = node_ref.shape
    edges = edge_ref.shape[0]
    nodes_all = rows * axis_count
    tile = 256

    def peer(step):
        return lax.rem(me + 2 * step, axis_count)

    def remote(src, dst, send, recv, to):
        return pltpu.make_async_remote_copy(
            src_ref=src,
            dst_ref=dst,
            send_sem=send,
            recv_sem=recv,
            device_id={"res": to},
            device_id_type=pl.DeviceIdType.MESH,
        )

    def nt(a, b):
        return lax.dot_general(a, b, (((1,), (1,)), ((), ())), preferred_element_type=f32)

    def nn(a, b):
        return jnp.dot(a, b, preferred_element_type=f32)

    def gather_copy(kind, buf, block, slot, to):
        return remote(
            buf.at[block], buf.at[block], all_send.at[kind, slot], all_recv.at[kind, block], to
        )

    def gather_start(kind, buf):
        def send(step, carry):
            gather_copy(kind, buf, me, step, peer(step)).start()
            return carry

        lax.fori_loop(1, chips, send, 0)
        gather_copy(kind, buf, me, 0, sibling).start()

    def gather_forward(kind, buf):
        def send(step, carry):
            block = peer(step)
            gather_copy(kind, buf, block, step, sibling).wait_recv()
            gather_copy(kind, buf, block, chips + step - 1, sibling).start()
            return carry

        lax.fori_loop(1, chips, send, 0)

    def gather_finish(kind, buf):
        def arrive(step, carry):
            block = lax.rem(sibling + 2 * step, axis_count)
            gather_copy(kind, buf, block, 0, sibling).wait_recv()
            return carry

        lax.fori_loop(0, chips, arrive, 0)

        def sent(slot, carry):
            gather_copy(kind, buf, me, slot, sibling).wait_send()
            return carry

        lax.fori_loop(0, 2 * chips - 1, sent, 0)

    def pair_copy(kind, buf, mid):
        return remote(buf.at[1 - core], mid, pair_send.at[kind], pair_recv.at[kind], sibling)

    def chip_copy(kind, own, into, other):
        return remote(
            own.at[other],
            into.at[chip],
            chip_send.at[kind, other],
            chip_recv.at[kind, chip],
            2 * other + core,
        )

    def reduce_mid(kind, buf, mid, own, into):
        pair_copy(kind, buf, mid).wait()

        def add(other, carry):
            own[other] = (buf[core, other].astype(f32) + mid[other].astype(f32)).astype(bf16)
            return carry

        lax.fori_loop(0, chips, add, 0)

        def send(step, carry):
            chip_copy(kind, own, into, lax.rem(chip + step, chips)).start()
            return carry

        lax.fori_loop(1, chips, send, 0)

    def reduce_end(kind, own, into):
        into[chip] = own[chip]

        def arrive(step, carry):
            other = lax.rem(chip + step, chips)
            remote(
                own.at[other],
                into.at[other],
                chip_send.at[kind, other],
                chip_recv.at[kind, other],
                2 * other + core,
            ).wait()
            return carry

        lax.fori_loop(1, chips, arrive, 0)
        total = into[0].astype(f32)
        for other in range(1, chips):
            total = total + into[other].astype(f32)
        return total

    barrier = pltpu.get_barrier_semaphore()

    def greet(step, carry):
        pl.semaphore_signal(
            barrier, inc=1, device_id={"res": peer(step)}, device_id_type=pl.DeviceIdType.MESH
        )
        return carry

    lax.fori_loop(1, chips, greet, 0)
    pl.semaphore_signal(
        barrier, inc=1, device_id={"res": sibling}, device_id_type=pl.DeviceIdType.MESH
    )
    table[me] = nn(node_ref[...], wnbr_ref[...]).astype(bf16)
    pl.semaphore_wait(barrier, chips)
    gather_start(0, table)

    def split(x):
        high = x.astype(bf16)
        return jnp.concatenate([high, (x - high.astype(f32)).astype(bf16)], axis=0)

    self_rep[...] = split(nn(node_ref[...], wself_ref[...]) + bias_ref[...])
    out_rep[...] = split(nt(gnode_ref[...], wnout_ref[...]) / nbr_count)

    def one_hot(mask):
        return jnp.where(mask, 1.0, 0.0).astype(bf16)

    def prepare(t, carry):
        start = pl.multiple_of(t * tile, tile)
        part = pl.ds(start, tile)
        picks[part, :] = one_hot(
            nbr_col_ref[part, :] == lax.broadcasted_iota(jnp.int32, (tile, nodes_all), 1)
        )
        row = lax.broadcasted_iota(jnp.int32, (tile, 2 * rows), 0) + start
        col = lax.broadcasted_iota(jnp.int32, (tile, 2 * rows), 1)
        first = jnp.where(col >= rows, col - rows, col) * nbr_count
        rep = one_hot((row >= first) & (row < first + nbr_count))
        base_pre[part, :] = nn(edge_ref[part, :], wedge_ref[...]) + nn(rep, self_rep[...])
        base_msg[part, :] = nt(gedge_ref[part, :], weout_ref[...]) + nn(rep, out_rep[...])
        return carry

    lax.fori_loop(0, edges // tile, prepare, 0)

    def prepare_t(t, carry):
        start = pl.multiple_of(t * tile, tile)
        picks_t[pl.ds(start, tile), :] = one_hot(
            nbr_row_ref[...] == lax.broadcasted_iota(jnp.int32, (tile, edges), 0) + start
        )
        return carry

    lax.fori_loop(0, nodes_all // tile, prepare_t, 0)
    first = lax.broadcasted_iota(jnp.int32, (rows, edges), 0) * nbr_count
    row = lax.broadcasted_iota(jnp.int32, (rows, edges), 1)
    own_t = one_hot((row >= first) & (row < first + nbr_count))

    gather_forward(0, table)
    gather_finish(0, table)

    def middle(t, carry):
        part = pl.ds(pl.multiple_of(t * tile, tile), tile)
        preact = base_pre[part, :] + nn(
            picks[part, :], table[...].reshape(nodes_all, table.shape[2])
        )
        values, slopes = gelu_parts(preact)
        msg_buf[part, :] = values.astype(bf16)
        pre_buf[part, :] = (base_msg[part, :] * slopes).astype(bf16)
        return carry

    lax.fori_loop(0, edges // tile, middle, 0)

    def spread(t, carry):
        part = pl.ds(pl.multiple_of(t * tile, tile), tile)
        found = nn(picks_t[part, :], pre_buf[...]).astype(bf16)
        for j in range(tile // rows):
            s_buf[j % 2, t * (tile // rows // 2) + j // 2] = found[j * rows : (j + 1) * rows]
        return carry

    lax.fori_loop(0, nodes_all // tile, spread, 0)
    pair_copy(0, s_buf, s_mid).start()

    pre_sum = nn(own_t, pre_buf[...]).astype(bf16)
    msg_sum = nn(own_t, msg_buf[...]).astype(bf16)

    def place(buf, at, value):
        count = value.shape[0] // axis_count
        for j in range(axis_count):
            buf[j % 2, j // 2, at : at + count, :] = value[j * count : (j + 1) * count].astype(bf16)

    hid = table.shape[2]
    own_self = width // axis_count
    own_hid = hid // axis_count
    place(w_buf, 0, contract_rows(node_ref[...], pre_sum))
    place(w_buf, own_self, contract_rows(edge_ref[...], pre_buf[...]))
    place(w_buf, own_self + own_hid, contract_rows(msg_buf[...], gedge_ref[...]))
    nout = contract_rows(msg_sum, gnode_ref[...]) / nbr_count
    place(w_buf, own_self + 2 * own_hid, nout[:, :hid])
    place(w_buf, own_self + 3 * own_hid, nout[:, hid:])
    pair_copy(1, w_buf, w_mid).start()

    reduce_mid(0, s_buf, s_mid, s_own, s_in)
    reduce_mid(1, w_buf, w_mid, w_own, w_in)

    def edge_out(t, carry):
        part = pl.ds(pl.multiple_of(t * tile, tile), tile)
        dedge_ref[part, :] = (
            nt(pre_buf[part, :], wedge_ref[...]) + gedge_ref[part, :].astype(f32)
        ).astype(bf16)
        return carry

    lax.fori_loop(0, edges // tile, edge_out, 0)

    reached = reduce_end(0, s_own, s_in)
    bias_sum = jnp.sum(reached, axis=0, keepdims=True)
    reached = reached.astype(bf16)
    place(n_buf, 0, contract_rows(node_ref[...], reached))
    pair_copy(2, n_buf, n_mid).start()
    dnode_ref[...] = (
        nt(pre_sum, wself_ref[...]) + nt(reached, wnbr_ref[...]) + gnode_ref[...].astype(f32)
    ).astype(bf16)
    reduce_mid(2, n_buf, n_mid, n_own, n_in)

    count = w_in.shape[1]
    w_all[me, 0:count, :] = reduce_end(1, w_own, w_in).astype(bf16)
    high = bias_sum.astype(bf16).astype(f32)
    line = lax.broadcasted_iota(jnp.int32, (16, hid), 0)
    w_all[me, count : count + 16, :] = jnp.where(
        line == 0, high, jnp.where(line == 1, bias_sum - high, 0.0)
    ).astype(bf16)
    gather_start(1, w_all)
    n_all[me] = reduce_end(2, n_own, n_in).astype(bf16)
    gather_start(2, n_all)
    gather_forward(1, w_all)
    gather_forward(2, n_all)
    gather_finish(1, w_all)

    def unpack(out, buf, at, size, cols):
        for j in range(axis_count):
            out[j * size : (j + 1) * size, cols] = buf[j, at : at + size, :]

    unpack(dself_ref, w_all, 0, own_self, slice(0, hid))
    unpack(dein_ref, w_all, own_self, own_hid, slice(0, hid))
    unpack(deout_ref, w_all, own_self + own_hid, own_hid, slice(0, hid))
    unpack(dnout_ref, w_all, own_self + 2 * own_hid, own_hid, slice(0, hid))
    unpack(dnout_ref, w_all, own_self + 3 * own_hid, own_hid, slice(hid, 2 * hid))
    total = w_all[0, count : count + 16, :].astype(f32)
    for j in range(1, axis_count):
        total = total + w_all[j, count : count + 16, :].astype(f32)
    dbias_ref[...] = jnp.sum(total, axis=0, keepdims=True)
    gather_finish(2, n_all)
    unpack(dnbr_ref, n_all, 0, own_self, slice(0, hid))


def fused(
    node_feats,
    edge_feats,
    neighbours,
    w_self,
    w_nbr,
    w_edge,
    bias,
    w_edge_out,
    w_node_out,
    grad_nodes,
    grad_edges,
):
    rows, nbr_count = neighbours.shape
    width, hid = w_self.shape
    edge_width = edge_feats.shape[2]
    edges = rows * nbr_count
    blocks = lax.axis_size("res")
    chips = blocks // 2
    nodes_all = rows * blocks
    own_w = (width + edge_width + hid + 2 * hid) // blocks
    own_n = width // blocks
    bf16, f32 = jnp.bfloat16, jnp.float32
    vmem = pl.BlockSpec(memory_space=pltpu.VMEM)

    def reduce_bufs(count):
        return [
            pltpu.VMEM((2, chips, count, hid), bf16),
            pltpu.VMEM((chips, count, hid), bf16),
            pltpu.VMEM((chips, count, hid), bf16),
            pltpu.VMEM((chips, count, hid), bf16),
        ]

    flops = 2 * edges * hid * (2 * nodes_all + 5 * edge_width)
    outs = pl.pallas_call(
        functools.partial(exchange_kernel, blocks, nbr_count),
        out_shape=(
            jax.ShapeDtypeStruct((rows, width), bf16),
            jax.ShapeDtypeStruct((edges, edge_width), bf16),
            jax.ShapeDtypeStruct((width, hid), bf16),
            jax.ShapeDtypeStruct((width, hid), bf16),
            jax.ShapeDtypeStruct((edge_width, hid), bf16),
            jax.ShapeDtypeStruct((1, hid), f32),
            jax.ShapeDtypeStruct((hid, edge_width), bf16),
            jax.ShapeDtypeStruct((hid, width), bf16),
        ),
        in_specs=[vmem] * 12,
        out_specs=[vmem] * 8,
        scratch_shapes=[
            pltpu.VMEM((blocks, rows, hid), bf16),
            pltpu.VMEM((edges, nodes_all), bf16),
            pltpu.VMEM((nodes_all, edges), bf16),
            pltpu.VMEM((edges, hid), f32),
            pltpu.VMEM((edges, hid), f32),
            pltpu.VMEM((edges, hid), bf16),
            pltpu.VMEM((edges, hid), bf16),
            pltpu.VMEM((2 * rows, hid), bf16),
            pltpu.VMEM((2 * rows, hid), bf16),
            *reduce_bufs(rows),
            *reduce_bufs(own_w),
            *reduce_bufs(own_n),
            pltpu.VMEM((blocks, own_w + 16, hid), bf16),
            pltpu.VMEM((blocks, own_n, hid), bf16),
            pltpu.SemaphoreType.DMA((3,)),
            pltpu.SemaphoreType.DMA((3,)),
            pltpu.SemaphoreType.DMA((3, chips)),
            pltpu.SemaphoreType.DMA((3, chips)),
            pltpu.SemaphoreType.DMA((3, blocks)),
            pltpu.SemaphoreType.DMA((3, blocks)),
        ],
        compiler_params=pltpu.CompilerParams(
            collective_id=0, has_side_effects=True, vmem_limit_bytes=40 * 1024 * 1024
        ),
        cost_estimate=pl.CostEstimate(flops=flops, bytes_accessed=8_000_000, transcendentals=edges * hid),
    )(
        node_feats,
        edge_feats.reshape(edges, edge_width),
        neighbours.reshape(edges, 1),
        neighbours.reshape(1, edges),
        w_self,
        w_nbr,
        w_edge,
        bias.reshape(1, hid),
        w_edge_out,
        w_node_out,
        grad_nodes,
        grad_edges.reshape(edges, edge_width),
    )
    d_nodes, d_edges, d_self, d_nbr, d_ein, d_bias, d_eout, d_nout = outs
    return (
        d_nodes,
        d_edges.reshape(rows, nbr_count, edge_width),
        d_self,
        d_nbr,
        d_ein,
        d_bias.reshape(hid),
        d_eout,
        d_nout,
    )


def local(
    node_feats,
    edge_feats,
    neighbours,
    w_self,
    w_nbr,
    w_edge,
    bias,
    w_edge_out,
    w_node_out,
    grad_nodes,
    grad_edges,
):
    res_rows = node_feats.shape[0]
    nbr_count = neighbours.shape[1]
    node_width = node_feats.shape[1]
    edge_width = edge_feats.shape[2]
    hidden = w_self.shape[1]
    edges_dev = res_rows * nbr_count
    blocks_res = lax.axis_size("res")
    nodes_all = res_rows * blocks_res
    edge_flat = edge_feats.reshape(edges_dev, edge_width)
    gedge_flat = grad_edges.reshape(edges_dev, edge_width)
    projected = jnp.dot(node_feats, w_nbr, preferred_element_type=jnp.float32).astype(jnp.bfloat16)
    table = lax.all_gather(projected, "res", axis=0, tiled=True)
    picks = (
        neighbours.reshape(-1)[:, None] == jnp.arange(nodes_all, dtype=jnp.int32)[None, :]
    ).astype(jnp.bfloat16)
    preact = (jnp.dot(node_feats, w_self, preferred_element_type=jnp.float32) + bias)[:, None, :]
    preact = preact + (
        jnp.dot(edge_flat, w_edge, preferred_element_type=jnp.float32)
        + jnp.dot(picks, table, preferred_element_type=jnp.float32)
    ).reshape(res_rows, nbr_count, hidden)
    values, slopes = gelu_parts(preact)
    message = values.astype(jnp.bfloat16)
    grad_msg = jnp.dot(gedge_flat, w_edge_out.T, preferred_element_type=jnp.float32).reshape(
        res_rows, nbr_count, hidden
    )
    grad_msg = (
        grad_msg
        + (jnp.dot(grad_nodes, w_node_out.T, preferred_element_type=jnp.float32) / nbr_count)[
            :, None, :
        ]
    )
    grad_pre = (grad_msg * slopes).astype(jnp.bfloat16)
    pre_flat = grad_pre.reshape(edges_dev, hidden)
    msg_flat = message.reshape(edges_dev, hidden)
    pre_sum = jnp.sum(grad_pre.astype(jnp.float32), axis=1).astype(jnp.bfloat16)
    msg_sum = jnp.sum(message.astype(jnp.float32), axis=1).astype(jnp.bfloat16)
    spread = contract_rows(picks, pre_flat).astype(jnp.bfloat16)
    landed = lax.all_to_all(
        spread.reshape(blocks_res, res_rows, hidden), "res", split_axis=0, concat_axis=0, tiled=True
    )
    reached = jnp.sum(landed.astype(jnp.float32), axis=0).astype(jnp.bfloat16)
    terms = (
        contract_rows(node_feats, pre_sum),
        contract_rows(node_feats, reached),
        contract_rows(edge_flat, pre_flat),
        contract_rows(msg_flat, gedge_flat),
        contract_rows(msg_sum, grad_nodes) / nbr_count,
    )
    packed = jnp.concatenate(
        [t.astype(jnp.bfloat16).reshape(blocks_res, -1, 128) for t in terms], axis=1
    )
    swapped = lax.all_to_all(packed, "res", split_axis=0, concat_axis=0, tiled=True)
    mine = jnp.sum(swapped.astype(jnp.float32), axis=0).astype(jnp.bfloat16)
    totals = lax.all_gather(mine, "res", axis=0, tiled=False)
    outs = []
    start = 0
    for t in terms:
        rows = t.size // blocks_res // 128
        outs.append(totals[:, start : start + rows].reshape(t.shape))
        start += rows
    grad_self, grad_nbr, grad_edge_in, grad_eout, grad_nout = outs
    grad_bias = lax.psum(jnp.sum(pre_flat.astype(jnp.float32), axis=0), "res")
    feat_index = lax.axis_index("feat")
    feat_count = lax.axis_size("feat")
    edge_part = edge_width // feat_count
    node_part = node_width // feat_count
    full_pre, full_wedge = (
        lax.all_gather(pre_flat, "feat", axis=1, tiled=True),
        lax.all_gather(w_edge, "feat", axis=1, tiled=True),
    )
    own_wedge = lax.dynamic_slice_in_dim(full_wedge, feat_index * edge_part, edge_part, 0)
    edge_summed = jnp.dot(full_pre, own_wedge.T, preferred_element_type=jnp.float32)
    gedge_part = lax.dynamic_slice_in_dim(gedge_flat, feat_index * edge_part, edge_part, 1).astype(
        jnp.float32
    )
    d_edges = (
        (edge_summed + gedge_part).astype(jnp.bfloat16).reshape(res_rows, nbr_count, edge_part)
    )
    node_total = jnp.dot(pre_sum, w_self.T, preferred_element_type=jnp.float32) + jnp.dot(
        reached, w_nbr.T, preferred_element_type=jnp.float32
    )
    node_total = lax.psum_scatter(node_total, "feat", scatter_dimension=1, tiled=True)
    gnode_part = lax.dynamic_slice_in_dim(grad_nodes, feat_index * node_part, node_part, 1).astype(
        jnp.float32
    )
    d_nodes = (node_total + gnode_part).astype(jnp.bfloat16)
    return (d_nodes, d_edges, grad_self, grad_nbr, grad_edge_in, grad_bias, grad_eout, grad_nout)


def solution(mesh):
    in_specs = (
        P(("groups", "res"), None),
        P(("groups", "res"), None, None),
        P(("groups", "res"), None),
        P(None, "feat"),
        P(None, "feat"),
        P(None, "feat"),
        P("feat"),
        P("feat", None),
        P("feat", None),
        P(("groups", "res"), None),
        P(("groups", "res"), None, None),
    )
    out_specs = (
        P(("groups", "res"), "feat"),
        P(("groups", "res"), None, "feat"),
        P("groups", "feat"),
        P("groups", "feat"),
        P("groups", "feat"),
        P(("groups", "feat")),
        P(("groups", "feat"), None),
        P(("groups", "feat"), None),
    )
    short = mesh.shape["res"] <= 16 and mesh.shape["feat"] == 1
    body = fused if short else local
    return jax.shard_map(body, mesh=mesh, in_specs=in_specs, out_specs=out_specs, check_vma=False)
```

```python
import functools

import jax
import jax.numpy as jnp
from jax import lax
from jax.experimental import pallas as pl
from jax.experimental.pallas import tpu as pltpu
from jax.sharding import PartitionSpec as P

gelu_scale = 0.7978845608028654
gelu_cubic = 0.044715


def gelu_parts(preact):
    inner = gelu_scale * (preact + gelu_cubic * preact * preact * preact)
    tangent = jnp.tanh(inner)
    values = 0.5 * preact * (1.0 + tangent)
    slopes = 0.5 * (1.0 + tangent) + 0.5 * preact * (1.0 - tangent * tangent) * gelu_scale * (
        1.0 + 3.0 * gelu_cubic * preact * preact
    )
    return (values, slopes)


def contract_rows(left, right):
    return lax.dot_general(
        left, right, (((0,), (0,)), ((), ())), preferred_element_type=jnp.float32
    )


def exchange_kernel(
    axis_count,
    nbr_count,
    node_hbm,
    edge_hbm,
    nbr_col_ref,
    nbr_row_ref,
    wself_hbm,
    wnbr_hbm,
    wedge_hbm,
    bias_ref,
    weout_hbm,
    wnout_hbm,
    gnode_hbm,
    gedge_hbm,
    dnode_ref,
    dedge_ref,
    dself_ref,
    dnbr_ref,
    dein_ref,
    dbias_ref,
    deout_ref,
    dnout_ref,
    node_ref,
    wself_ref,
    wnbr_ref,
    wedge_ref,
    weout_ref,
    wnout_ref,
    gnode_ref,
    edge_ref,
    gedge_ref,
    in_sem,
    table,
    picks,
    picks_t,
    base_pre,
    base_msg,
    pre_buf,
    msg_buf,
    self_rep,
    out_rep,
    s_buf,
    s_mid,
    s_own,
    s_in,
    w_buf,
    w_mid,
    w_own,
    w_in,
    n_buf,
    n_mid,
    n_own,
    n_in,
    w_all,
    n_all,
    pair_send,
    pair_recv,
    chip_send,
    chip_recv,
    all_send,
    all_recv,
):
    f32, bf16 = jnp.float32, jnp.bfloat16
    chips = axis_count // 2
    me = lax.axis_index("res")
    core = lax.rem(me, 2)
    chip = lax.div(me, 2)
    sibling = me + 1 - 2 * core
    rows, width = node_ref.shape
    edges = edge_ref.shape[0]
    nodes_all = rows * axis_count
    tile = 256

    def peer(step):
        return lax.rem(me + 2 * step, axis_count)

    def remote(src, dst, send, recv, to):
        return pltpu.make_async_remote_copy(
            src_ref=src,
            dst_ref=dst,
            send_sem=send,
            recv_sem=recv,
            device_id={"res": to},
            device_id_type=pl.DeviceIdType.MESH,
        )

    def nt(a, b):
        return lax.dot_general(a, b, (((1,), (1,)), ((), ())), preferred_element_type=f32)

    def nn(a, b):
        return jnp.dot(a, b, preferred_element_type=f32)

    def gather_copy(kind, buf, block, slot, to):
        return remote(
            buf.at[block], buf.at[block], all_send.at[kind, slot], all_recv.at[kind, block], to
        )

    across = 4 * lax.div(me, 4) + lax.rem(me + 2, 4)
    planes = axis_count // 4

    def gather_start(kind, buf):
        def send(step, carry):
            gather_copy(kind, buf, me, step, peer(2 * step)).start()
            return carry

        lax.fori_loop(1, planes, send, 0)
        gather_copy(kind, buf, me, planes, across).start()
        gather_copy(kind, buf, me, 0, sibling).start()

    def gather_forward(kind, buf):
        def along(step, carry):
            block = peer(2 * step)
            gather_copy(kind, buf, block, 0, sibling).wait_recv()
            gather_copy(kind, buf, block, planes + step, across).start()
            gather_copy(kind, buf, block, 2 * planes + step - 1, sibling).start()
            return carry

        lax.fori_loop(1, planes, along, 0)

        def over(step, carry):
            block = lax.rem(across + 4 * step, axis_count)
            gather_copy(kind, buf, block, 0, sibling).wait_recv()
            gather_copy(kind, buf, block, 3 * planes + step - 1, sibling).start()
            return carry

        lax.fori_loop(0, planes, over, 0)

    def gather_finish(kind, buf):
        def arrive(step, carry):
            block = lax.rem(sibling + 2 * step, axis_count)
            gather_copy(kind, buf, block, 0, sibling).wait_recv()
            return carry

        lax.fori_loop(0, chips, arrive, 0)

        def sent(slot, carry):
            gather_copy(kind, buf, me, slot, sibling).wait_send()
            return carry

        lax.fori_loop(0, 2 * chips - 1, sent, 0)

    def pair_copy(kind, buf, mid):
        return remote(buf.at[1 - core], mid, pair_send.at[kind], pair_recv.at[kind], sibling)

    def chip_copy(kind, own, into, other):
        return remote(
            own.at[other],
            into.at[chip],
            chip_send.at[kind, other],
            chip_recv.at[kind, chip],
            2 * other + core,
        )

    def reduce_mid(kind, buf, mid, own, into):
        pair_copy(kind, buf, mid).wait()

        def add(other, carry):
            own[other] = (buf[core, other].astype(f32) + mid[other].astype(f32)).astype(bf16)
            return carry

        lax.fori_loop(0, chips, add, 0)

        def send(step, carry):
            chip_copy(kind, own, into, lax.rem(chip + step, chips)).start()
            return carry

        lax.fori_loop(1, chips, send, 0)

    def reduce_end(kind, own, into):
        into[chip] = own[chip]

        def arrive(step, carry):
            other = lax.rem(chip + step, chips)
            remote(
                own.at[other],
                into.at[other],
                chip_send.at[kind, other],
                chip_recv.at[kind, other],
                2 * other + core,
            ).wait()
            return carry

        lax.fori_loop(1, chips, arrive, 0)
        total = into[0].astype(f32)
        for other in range(1, chips):
            total = total + into[other].astype(f32)
        return total

    loads = [
        pltpu.make_async_copy(source, target, in_sem.at[slot])
        for slot, (source, target) in enumerate(
            [
                (node_hbm, node_ref),
                (wnbr_hbm, wnbr_ref),
                (wself_hbm, wself_ref),
                (gnode_hbm, gnode_ref),
                (wnout_hbm, wnout_ref),
                (wedge_hbm, wedge_ref),
                (weout_hbm, weout_ref),
                (edge_hbm, edge_ref),
                (gedge_hbm, gedge_ref),
            ]
        )
    ]
    for load in loads:
        load.start()
    barrier = pltpu.get_barrier_semaphore()

    def greet(step, carry):
        pl.semaphore_signal(
            barrier, inc=1, device_id={"res": peer(step)}, device_id_type=pl.DeviceIdType.MESH
        )
        return carry

    lax.fori_loop(1, chips, greet, 0)
    pl.semaphore_signal(
        barrier, inc=1, device_id={"res": sibling}, device_id_type=pl.DeviceIdType.MESH
    )
    loads[0].wait()
    loads[1].wait()
    table[me] = nn(node_ref[...], wnbr_ref[...]).astype(bf16)
    pl.semaphore_wait(barrier, chips)
    gather_start(0, table)
    for load in loads[2:]:
        load.wait()

    def split(x):
        high = x.astype(bf16)
        return jnp.concatenate([high, (x - high.astype(f32)).astype(bf16)], axis=0)

    self_rep[...] = split(nn(node_ref[...], wself_ref[...]) + bias_ref[...])
    out_rep[...] = split(nt(gnode_ref[...], wnout_ref[...]) / nbr_count)

    def one_hot(mask):
        return jnp.where(mask, 1.0, 0.0).astype(bf16)

    def prepare(t, carry):
        start = pl.multiple_of(t * tile, tile)
        part = pl.ds(start, tile)
        picks[part, :] = one_hot(
            nbr_col_ref[part, :] == lax.broadcasted_iota(jnp.int32, (tile, nodes_all), 1)
        )
        row = lax.broadcasted_iota(jnp.int32, (tile, 2 * rows), 0)
        col = lax.broadcasted_iota(jnp.int32, (tile, 2 * rows), 1)
        rep = one_hot(row & (rows - 1) == col & (rows - 1))
        base_pre[part, :] = nn(edge_ref[part, :], wedge_ref[...]) + nn(rep, self_rep[...])
        base_msg[part, :] = nt(gedge_ref[part, :], weout_ref[...]) + nn(rep, out_rep[...])
        return carry

    lax.fori_loop(0, edges // tile, prepare, 0)

    def prepare_t(t, carry):
        start = pl.multiple_of(t * tile, tile)
        picks_t[pl.ds(start, tile), :] = one_hot(
            nbr_row_ref[...] == lax.broadcasted_iota(jnp.int32, (tile, edges), 0) + start
        )
        return carry

    lax.fori_loop(0, nodes_all // tile, prepare_t, 0)
    row = lax.broadcasted_iota(jnp.int32, (rows, edges), 0)
    col = lax.broadcasted_iota(jnp.int32, (rows, edges), 1)
    own_t = one_hot(col & (rows - 1) == row)

    gather_forward(0, table)
    gather_finish(0, table)

    def middle(t, carry):
        part = pl.ds(pl.multiple_of(t * tile, tile), tile)
        preact = base_pre[part, :] + nn(
            picks[part, :], table[...].reshape(nodes_all, table.shape[2])
        )
        values, slopes = gelu_parts(preact)
        msg_buf[part, :] = values.astype(bf16)
        pre_buf[part, :] = (base_msg[part, :] * slopes).astype(bf16)
        return carry

    lax.fori_loop(0, edges // tile, middle, 0)

    def spread(t, carry):
        part = pl.ds(pl.multiple_of(t * tile, tile), tile)
        found = nn(picks_t[part, :], pre_buf[...]).astype(bf16)
        for j in range(tile // rows):
            s_buf[j % 2, t * (tile // rows // 2) + j // 2] = found[j * rows : (j + 1) * rows]
        return carry

    lax.fori_loop(0, nodes_all // tile, spread, 0)
    pair_copy(0, s_buf, s_mid).start()

    pre_sum = nn(own_t, pre_buf[...]).astype(bf16)
    msg_sum = nn(own_t, msg_buf[...]).astype(bf16)

    def place(buf, at, value):
        count = value.shape[0] // axis_count
        for j in range(axis_count):
            buf[j % 2, j // 2, at : at + count, :] = value[j * count : (j + 1) * count].astype(bf16)

    hid = table.shape[2]
    own_self = width // axis_count
    own_hid = hid // axis_count
    place(w_buf, 0, contract_rows(node_ref[...], pre_sum))
    place(w_buf, own_self, contract_rows(edge_ref[...], pre_buf[...]))
    place(w_buf, own_self + own_hid, contract_rows(msg_buf[...], gedge_ref[...]))
    nout = contract_rows(msg_sum, gnode_ref[...]) / nbr_count
    place(w_buf, own_self + 2 * own_hid, nout[:, :hid])
    place(w_buf, own_self + 3 * own_hid, nout[:, hid:])
    pair_copy(1, w_buf, w_mid).start()

    reduce_mid(0, s_buf, s_mid, s_own, s_in)
    reduce_mid(1, w_buf, w_mid, w_own, w_in)

    def edge_out(t, carry):
        part = pl.ds(pl.multiple_of(t * tile, tile), tile)
        dedge_ref[part, :] = (
            nt(pre_buf[part, :], wedge_ref[...]) + gedge_ref[part, :].astype(f32)
        ).astype(bf16)
        return carry

    lax.fori_loop(0, edges // tile, edge_out, 0)

    reached = reduce_end(0, s_own, s_in)
    bias_sum = jnp.sum(reached, axis=0, keepdims=True)
    reached = reached.astype(bf16)
    place(n_buf, 0, contract_rows(node_ref[...], reached))
    pair_copy(2, n_buf, n_mid).start()
    dnode_ref[...] = (
        nt(pre_sum, wself_ref[...]) + nt(reached, wnbr_ref[...]) + gnode_ref[...].astype(f32)
    ).astype(bf16)
    reduce_mid(2, n_buf, n_mid, n_own, n_in)

    count = w_in.shape[1]
    w_all[me, 0:count, :] = reduce_end(1, w_own, w_in).astype(bf16)
    high = bias_sum.astype(bf16).astype(f32)
    line = lax.broadcasted_iota(jnp.int32, (16, hid), 0)
    w_all[me, count : count + 16, :] = jnp.where(
        line == 0, high, jnp.where(line == 1, bias_sum - high, 0.0)
    ).astype(bf16)
    gather_start(1, w_all)
    n_all[me] = reduce_end(2, n_own, n_in).astype(bf16)
    gather_start(2, n_all)
    gather_forward(1, w_all)
    gather_forward(2, n_all)
    gather_finish(1, w_all)

    def unpack(out, buf, at, size, cols):
        for j in range(axis_count):
            out[j * size : (j + 1) * size, cols] = buf[j, at : at + size, :]

    unpack(dself_ref, w_all, 0, own_self, slice(0, hid))
    unpack(dein_ref, w_all, own_self, own_hid, slice(0, hid))
    unpack(deout_ref, w_all, own_self + own_hid, own_hid, slice(0, hid))
    unpack(dnout_ref, w_all, own_self + 2 * own_hid, own_hid, slice(0, hid))
    unpack(dnout_ref, w_all, own_self + 3 * own_hid, own_hid, slice(hid, 2 * hid))
    total = w_all[0, count : count + 16, :].astype(f32)
    for j in range(1, axis_count):
        total = total + w_all[j, count : count + 16, :].astype(f32)
    dbias_ref[...] = jnp.sum(total, axis=0, keepdims=True)
    gather_finish(2, n_all)
    unpack(dnbr_ref, n_all, 0, own_self, slice(0, hid))


def store_kernel(*refs):
    count = len(refs) // 2
    sems = refs[-1]
    copies = [
        pltpu.make_async_copy(refs[slot], refs[count + slot], sems.at[slot]) for slot in range(count)
    ]
    for copy in copies:
        copy.start()
    for copy in copies:
        copy.wait()


def fused(
    node_feats,
    edge_feats,
    neighbours,
    w_self,
    w_nbr,
    w_edge,
    bias,
    w_edge_out,
    w_node_out,
    grad_nodes,
    grad_edges,
):
    rows, nbr_count = neighbours.shape
    width, hid = w_self.shape
    edge_width = edge_feats.shape[2]
    edges = rows * nbr_count
    blocks = lax.axis_size("res")
    chips = blocks // 2
    nodes_all = rows * blocks
    own_w = (width + edge_width + hid + 2 * hid) // blocks
    own_n = width // blocks
    bf16, f32 = jnp.bfloat16, jnp.float32
    vmem = pl.BlockSpec(memory_space=pltpu.VMEM)
    hbm = pl.BlockSpec(memory_space=pl.ANY)

    def reduce_bufs(count):
        return [
            pltpu.VMEM((2, chips, count, hid), bf16),
            pltpu.VMEM((chips, count, hid), bf16),
            pltpu.VMEM((chips, count, hid), bf16),
            pltpu.VMEM((chips, count, hid), bf16),
        ]

    flops = 2 * edges * hid * (2 * nodes_all + 5 * edge_width)
    outs = pl.pallas_call(
        functools.partial(exchange_kernel, blocks, nbr_count),
        out_shape=(
            jax.ShapeDtypeStruct((rows, width), bf16),
            jax.ShapeDtypeStruct((edges, edge_width), bf16),
            jax.ShapeDtypeStruct((width, hid), bf16),
            jax.ShapeDtypeStruct((width, hid), bf16),
            jax.ShapeDtypeStruct((edge_width, hid), bf16),
            jax.ShapeDtypeStruct((1, hid), f32),
            jax.ShapeDtypeStruct((hid, edge_width), bf16),
            jax.ShapeDtypeStruct((hid, width), bf16),
        ),
        in_specs=[hbm, hbm, vmem, vmem, hbm, hbm, hbm, vmem, hbm, hbm, hbm, hbm],
        out_specs=[vmem] * 8,
        scratch_shapes=[
            pltpu.VMEM((rows, width), bf16),
            pltpu.VMEM((width, hid), bf16),
            pltpu.VMEM((width, hid), bf16),
            pltpu.VMEM((edge_width, hid), bf16),
            pltpu.VMEM((hid, edge_width), bf16),
            pltpu.VMEM((hid, width), bf16),
            pltpu.VMEM((rows, width), bf16),
            pltpu.VMEM((edges, edge_width), bf16),
            pltpu.VMEM((edges, edge_width), bf16),
            pltpu.SemaphoreType.DMA((9,)),
            pltpu.VMEM((blocks, rows, hid), bf16),
            pltpu.VMEM((edges, nodes_all), bf16),
            pltpu.VMEM((nodes_all, edges), bf16),
            pltpu.VMEM((edges, hid), f32),
            pltpu.VMEM((edges, hid), f32),
            pltpu.VMEM((edges, hid), bf16),
            pltpu.VMEM((edges, hid), bf16),
            pltpu.VMEM((2 * rows, hid), bf16),
            pltpu.VMEM((2 * rows, hid), bf16),
            *reduce_bufs(rows),
            *reduce_bufs(own_w),
            *reduce_bufs(own_n),
            pltpu.VMEM((blocks, own_w + 16, hid), bf16),
            pltpu.VMEM((blocks, own_n, hid), bf16),
            pltpu.SemaphoreType.DMA((3,)),
            pltpu.SemaphoreType.DMA((3,)),
            pltpu.SemaphoreType.DMA((3, chips)),
            pltpu.SemaphoreType.DMA((3, chips)),
            pltpu.SemaphoreType.DMA((3, blocks)),
            pltpu.SemaphoreType.DMA((3, blocks)),
        ],
        compiler_params=pltpu.CompilerParams(
            collective_id=0, has_side_effects=True, vmem_limit_bytes=58 * 1024 * 1024
        ),
        cost_estimate=pl.CostEstimate(flops=flops, bytes_accessed=8_000_000, transcendentals=edges * hid),
    )(
        node_feats,
        edge_feats.transpose(1, 0, 2).reshape(edges, edge_width),
        neighbours.T.reshape(edges, 1),
        neighbours.T.reshape(1, edges),
        w_self,
        w_nbr,
        w_edge,
        bias.reshape(1, hid),
        w_edge_out,
        w_node_out,
        grad_nodes,
        grad_edges.transpose(1, 0, 2).reshape(edges, edge_width),
    )
    count = len(outs)
    outs = pl.pallas_call(
        store_kernel,
        out_shape=tuple(jax.ShapeDtypeStruct(x.shape, x.dtype) for x in outs),
        in_specs=[hbm] * count,
        out_specs=[hbm] * count,
        scratch_shapes=[pltpu.SemaphoreType.DMA((count,))],
        compiler_params=pltpu.CompilerParams(vmem_limit_bytes=58 * 1024 * 1024),
    )(*outs)
    d_nodes, d_edges, d_self, d_nbr, d_ein, d_bias, d_eout, d_nout = outs
    return (
        d_nodes,
        d_edges.reshape(nbr_count, rows, edge_width).transpose(1, 0, 2),
        d_self,
        d_nbr,
        d_ein,
        d_bias.reshape(hid),
        d_eout,
        d_nout,
    )


def local(
    node_feats,
    edge_feats,
    neighbours,
    w_self,
    w_nbr,
    w_edge,
    bias,
    w_edge_out,
    w_node_out,
    grad_nodes,
    grad_edges,
):
    res_rows = node_feats.shape[0]
    nbr_count = neighbours.shape[1]
    node_width = node_feats.shape[1]
    edge_width = edge_feats.shape[2]
    hidden = w_self.shape[1]
    edges_dev = res_rows * nbr_count
    blocks_res = lax.axis_size("res")
    nodes_all = res_rows * blocks_res
    edge_flat = edge_feats.reshape(edges_dev, edge_width)
    gedge_flat = grad_edges.reshape(edges_dev, edge_width)
    projected = jnp.dot(node_feats, w_nbr, preferred_element_type=jnp.float32).astype(jnp.bfloat16)
    table = lax.all_gather(projected, "res", axis=0, tiled=True)
    picks = (
        neighbours.reshape(-1)[:, None] == jnp.arange(nodes_all, dtype=jnp.int32)[None, :]
    ).astype(jnp.bfloat16)
    preact = (jnp.dot(node_feats, w_self, preferred_element_type=jnp.float32) + bias)[:, None, :]
    preact = preact + (
        jnp.dot(edge_flat, w_edge, preferred_element_type=jnp.float32)
        + jnp.dot(picks, table, preferred_element_type=jnp.float32)
    ).reshape(res_rows, nbr_count, hidden)
    values, slopes = gelu_parts(preact)
    message = values.astype(jnp.bfloat16)
    grad_msg = jnp.dot(gedge_flat, w_edge_out.T, preferred_element_type=jnp.float32).reshape(
        res_rows, nbr_count, hidden
    )
    grad_msg = (
        grad_msg
        + (jnp.dot(grad_nodes, w_node_out.T, preferred_element_type=jnp.float32) / nbr_count)[
            :, None, :
        ]
    )
    grad_pre = (grad_msg * slopes).astype(jnp.bfloat16)
    pre_flat = grad_pre.reshape(edges_dev, hidden)
    msg_flat = message.reshape(edges_dev, hidden)
    pre_sum = jnp.sum(grad_pre.astype(jnp.float32), axis=1).astype(jnp.bfloat16)
    msg_sum = jnp.sum(message.astype(jnp.float32), axis=1).astype(jnp.bfloat16)
    spread = contract_rows(picks, pre_flat).astype(jnp.bfloat16)
    landed = lax.all_to_all(
        spread.reshape(blocks_res, res_rows, hidden), "res", split_axis=0, concat_axis=0, tiled=True
    )
    reached = jnp.sum(landed.astype(jnp.float32), axis=0).astype(jnp.bfloat16)
    terms = (
        contract_rows(node_feats, pre_sum),
        contract_rows(node_feats, reached),
        contract_rows(edge_flat, pre_flat),
        contract_rows(msg_flat, gedge_flat),
        contract_rows(msg_sum, grad_nodes) / nbr_count,
    )
    packed = jnp.concatenate(
        [t.astype(jnp.bfloat16).reshape(blocks_res, -1, 128) for t in terms], axis=1
    )
    swapped = lax.all_to_all(packed, "res", split_axis=0, concat_axis=0, tiled=True)
    mine = jnp.sum(swapped.astype(jnp.float32), axis=0).astype(jnp.bfloat16)
    totals = lax.all_gather(mine, "res", axis=0, tiled=False)
    outs = []
    start = 0
    for t in terms:
        rows = t.size // blocks_res // 128
        outs.append(totals[:, start : start + rows].reshape(t.shape))
        start += rows
    grad_self, grad_nbr, grad_edge_in, grad_eout, grad_nout = outs
    grad_bias = lax.psum(jnp.sum(pre_flat.astype(jnp.float32), axis=0), "res")
    feat_index = lax.axis_index("feat")
    feat_count = lax.axis_size("feat")
    edge_part = edge_width // feat_count
    node_part = node_width // feat_count
    full_pre, full_wedge = (
        lax.all_gather(pre_flat, "feat", axis=1, tiled=True),
        lax.all_gather(w_edge, "feat", axis=1, tiled=True),
    )
    own_wedge = lax.dynamic_slice_in_dim(full_wedge, feat_index * edge_part, edge_part, 0)
    edge_summed = jnp.dot(full_pre, own_wedge.T, preferred_element_type=jnp.float32)
    gedge_part = lax.dynamic_slice_in_dim(gedge_flat, feat_index * edge_part, edge_part, 1).astype(
        jnp.float32
    )
    d_edges = (
        (edge_summed + gedge_part).astype(jnp.bfloat16).reshape(res_rows, nbr_count, edge_part)
    )
    node_total = jnp.dot(pre_sum, w_self.T, preferred_element_type=jnp.float32) + jnp.dot(
        reached, w_nbr.T, preferred_element_type=jnp.float32
    )
    node_total = lax.psum_scatter(node_total, "feat", scatter_dimension=1, tiled=True)
    gnode_part = lax.dynamic_slice_in_dim(grad_nodes, feat_index * node_part, node_part, 1).astype(
        jnp.float32
    )
    d_nodes = (node_total + gnode_part).astype(jnp.bfloat16)
    return (d_nodes, d_edges, grad_self, grad_nbr, grad_edge_in, grad_bias, grad_eout, grad_nout)


def solution(mesh):
    in_specs = (
        P(("groups", "res"), None),
        P(("groups", "res"), None, None),
        P(("groups", "res"), None),
        P(None, "feat"),
        P(None, "feat"),
        P(None, "feat"),
        P("feat"),
        P("feat", None),
        P("feat", None),
        P(("groups", "res"), None),
        P(("groups", "res"), None, None),
    )
    out_specs = (
        P(("groups", "res"), "feat"),
        P(("groups", "res"), None, "feat"),
        P("groups", "feat"),
        P("groups", "feat"),
        P("groups", "feat"),
        P(("groups", "feat")),
        P(("groups", "feat"), None),
        P(("groups", "feat"), None),
    )
    short = mesh.shape["res"] == 16 and mesh.shape["feat"] == 1
    body = fused if short else local
    return jax.shard_map(body, mesh=mesh, in_specs=in_specs, out_specs=out_specs, check_vma=False)
```

```python
import functools

import jax
import jax.numpy as jnp
from jax import lax
from jax.experimental import pallas as pl
from jax.experimental.pallas import tpu as pltpu
from jax.sharding import PartitionSpec as P

gelu_scale = 0.7978845608028654
gelu_cubic = 0.044715


def gelu_parts(preact):
    inner = gelu_scale * (preact + gelu_cubic * preact * preact * preact)
    tangent = jnp.tanh(inner)
    values = 0.5 * preact * (1.0 + tangent)
    slopes = 0.5 * (1.0 + tangent) + 0.5 * preact * (1.0 - tangent * tangent) * gelu_scale * (
        1.0 + 3.0 * gelu_cubic * preact * preact
    )
    return (values, slopes)


def contract_rows(left, right):
    return lax.dot_general(
        left, right, (((0,), (0,)), ((), ())), preferred_element_type=jnp.float32
    )


def exchange_kernel(
    axis_count,
    nbr_count,
    node_hbm,
    edge_hbm,
    nbr_col_ref,
    nbr_row_ref,
    wself_hbm,
    wnbr_hbm,
    wedge_hbm,
    bias_ref,
    weout_hbm,
    wnout_hbm,
    gnode_hbm,
    gedge_hbm,
    dnode_ref,
    dedge_ref,
    dself_ref,
    dnbr_ref,
    dein_ref,
    dbias_ref,
    deout_ref,
    dnout_ref,
    node_ref,
    wself_ref,
    wnbr_ref,
    wedge_ref,
    weout_ref,
    wnout_ref,
    gnode_ref,
    edge_ref,
    gedge_ref,
    in_sem,
    table,
    picks,
    picks_t,
    base_pre,
    base_msg,
    pre_buf,
    msg_buf,
    self_rep,
    out_rep,
    s_buf,
    s_mid,
    s_own,
    s_in,
    w_buf,
    w_mid,
    w_own,
    w_in,
    n_buf,
    n_mid,
    n_own,
    n_in,
    w_all,
    n_all,
    pair_send,
    pair_recv,
    chip_send,
    chip_recv,
    all_send,
    all_recv,
):
    f32, bf16 = jnp.float32, jnp.bfloat16
    chips = axis_count // 2
    me = lax.axis_index("res")
    core = lax.rem(me, 2)
    chip = lax.div(me, 2)
    sibling = me + 1 - 2 * core
    rows, width = node_ref.shape
    edges = edge_ref.shape[0]
    nodes_all = rows * axis_count
    tile = 256

    def peer(step):
        return lax.rem(me + 2 * step, axis_count)

    def remote(src, dst, send, recv, to):
        return pltpu.make_async_remote_copy(
            src_ref=src,
            dst_ref=dst,
            send_sem=send,
            recv_sem=recv,
            device_id={"res": to},
            device_id_type=pl.DeviceIdType.MESH,
        )

    def nt(a, b):
        return lax.dot_general(a, b, (((1,), (1,)), ((), ())), preferred_element_type=f32)

    def nn(a, b):
        return jnp.dot(a, b, preferred_element_type=f32)

    def gather_copy(kind, buf, block, slot, to):
        return remote(
            buf.at[block], buf.at[block], all_send.at[kind, slot], all_recv.at[kind, block], to
        )

    across = 4 * lax.div(me, 4) + lax.rem(me + 2, 4)
    planes = axis_count // 4

    def gather_start(kind, buf):
        def send(step, carry):
            gather_copy(kind, buf, me, step, peer(2 * step)).start()
            return carry

        lax.fori_loop(1, planes, send, 0)
        gather_copy(kind, buf, me, planes, across).start()
        gather_copy(kind, buf, me, 0, sibling).start()

    def gather_forward(kind, buf):
        def along(step, carry):
            block = peer(2 * step)
            gather_copy(kind, buf, block, 0, sibling).wait_recv()
            gather_copy(kind, buf, block, planes + step, across).start()
            gather_copy(kind, buf, block, 2 * planes + step - 1, sibling).start()
            return carry

        lax.fori_loop(1, planes, along, 0)

        def over(step, carry):
            block = lax.rem(across + 4 * step, axis_count)
            gather_copy(kind, buf, block, 0, sibling).wait_recv()
            gather_copy(kind, buf, block, 3 * planes + step - 1, sibling).start()
            return carry

        lax.fori_loop(0, planes, over, 0)

    def gather_finish(kind, buf):
        def arrive(step, carry):
            block = lax.rem(sibling + 2 * step, axis_count)
            gather_copy(kind, buf, block, 0, sibling).wait_recv()
            return carry

        lax.fori_loop(0, chips, arrive, 0)

        def sent(slot, carry):
            gather_copy(kind, buf, me, slot, sibling).wait_send()
            return carry

        lax.fori_loop(0, 2 * chips - 1, sent, 0)

    def pair_copy(kind, buf, mid):
        return remote(buf.at[1 - core], mid, pair_send.at[kind], pair_recv.at[kind], sibling)

    def chip_copy(kind, own, into, other):
        return remote(
            own.at[other],
            into.at[chip],
            chip_send.at[kind, other],
            chip_recv.at[kind, chip],
            2 * other + core,
        )

    def reduce_mid(kind, buf, mid, own, into):
        pair_copy(kind, buf, mid).wait()

        def add(other, carry):
            own[other] = (buf[core, other].astype(f32) + mid[other].astype(f32)).astype(bf16)
            return carry

        lax.fori_loop(0, chips, add, 0)

        def send(step, carry):
            chip_copy(kind, own, into, lax.rem(chip + step, chips)).start()
            return carry

        lax.fori_loop(1, chips, send, 0)

    def reduce_end(kind, own, into):
        into[chip] = own[chip]

        def arrive(step, carry):
            other = lax.rem(chip + step, chips)
            remote(
                own.at[other],
                into.at[other],
                chip_send.at[kind, other],
                chip_recv.at[kind, other],
                2 * other + core,
            ).wait()
            return carry

        lax.fori_loop(1, chips, arrive, 0)
        total = into[0].astype(f32)
        for other in range(1, chips):
            total = total + into[other].astype(f32)
        return total

    loads = [
        pltpu.make_async_copy(source, target, in_sem.at[slot])
        for slot, (source, target) in enumerate(
            [
                (node_hbm, node_ref),
                (wnbr_hbm, wnbr_ref),
                (wself_hbm, wself_ref),
                (gnode_hbm, gnode_ref),
                (wnout_hbm, wnout_ref),
                (wedge_hbm, wedge_ref),
                (weout_hbm, weout_ref),
                (edge_hbm, edge_ref),
                (gedge_hbm, gedge_ref),
            ]
        )
    ]
    for load in loads:
        load.start()
    barrier = pltpu.get_barrier_semaphore()

    def greet(step, carry):
        pl.semaphore_signal(
            barrier, inc=1, device_id={"res": peer(step)}, device_id_type=pl.DeviceIdType.MESH
        )
        return carry

    lax.fori_loop(1, chips, greet, 0)
    pl.semaphore_signal(
        barrier, inc=1, device_id={"res": sibling}, device_id_type=pl.DeviceIdType.MESH
    )
    loads[0].wait()
    loads[1].wait()
    table[me] = nn(node_ref[...], wnbr_ref[...]).astype(bf16)
    pl.semaphore_wait(barrier, chips)
    gather_start(0, table)
    for load in loads[2:]:
        load.wait()

    def split(x):
        high = x.astype(bf16)
        return jnp.concatenate([high, (x - high.astype(f32)).astype(bf16)], axis=0)

    self_rep[...] = split(nn(node_ref[...], wself_ref[...]) + bias_ref[...])
    out_rep[...] = split(nt(gnode_ref[...], wnout_ref[...]) / nbr_count)

    def one_hot(mask):
        return jnp.where(mask, 1.0, 0.0).astype(bf16)

    def prepare(t, carry):
        start = pl.multiple_of(t * tile, tile)
        part = pl.ds(start, tile)
        picks[part, :] = one_hot(
            nbr_col_ref[part, :] == lax.broadcasted_iota(jnp.int32, (tile, nodes_all), 1)
        )
        row = lax.broadcasted_iota(jnp.int32, (tile, 2 * rows), 0)
        col = lax.broadcasted_iota(jnp.int32, (tile, 2 * rows), 1)
        rep = one_hot(row & (rows - 1) == col & (rows - 1))
        base_pre[part, :] = nn(edge_ref[part, :], wedge_ref[...]) + nn(rep, self_rep[...])
        base_msg[part, :] = nt(gedge_ref[part, :], weout_ref[...]) + nn(rep, out_rep[...])
        return carry

    lax.fori_loop(0, edges // tile, prepare, 0)

    def prepare_t(t, carry):
        start = pl.multiple_of(t * tile, tile)
        picks_t[pl.ds(start, tile), :] = one_hot(
            nbr_row_ref[...] == lax.broadcasted_iota(jnp.int32, (tile, edges), 0) + start
        )
        return carry

    lax.fori_loop(0, nodes_all // tile, prepare_t, 0)
    row = lax.broadcasted_iota(jnp.int32, (rows, edges), 0)
    col = lax.broadcasted_iota(jnp.int32, (rows, edges), 1)
    own_t = one_hot(col & (rows - 1) == row)

    gather_forward(0, table)
    gather_finish(0, table)

    def middle(t, carry):
        part = pl.ds(pl.multiple_of(t * tile, tile), tile)
        preact = base_pre[part, :] + nn(
            picks[part, :], table[...].reshape(nodes_all, table.shape[2])
        )
        values, slopes = gelu_parts(preact)
        msg_buf[part, :] = values.astype(bf16)
        pre_buf[part, :] = (base_msg[part, :] * slopes).astype(bf16)
        return carry

    lax.fori_loop(0, edges // tile, middle, 0)

    def spread(t, carry):
        part = pl.ds(pl.multiple_of(t * tile, tile), tile)
        found = nn(picks_t[part, :], pre_buf[...]).astype(bf16)
        for j in range(tile // rows):
            s_buf[j % 2, t * (tile // rows // 2) + j // 2] = found[j * rows : (j + 1) * rows]
        return carry

    lax.fori_loop(0, nodes_all // tile, spread, 0)
    pair_copy(0, s_buf, s_mid).start()

    pre_sum = nn(own_t, pre_buf[...]).astype(bf16)
    msg_sum = nn(own_t, msg_buf[...]).astype(bf16)

    def place(buf, at, value):
        count = value.shape[0] // axis_count
        for j in range(axis_count):
            buf[j % 2, j // 2, at : at + count, :] = value[j * count : (j + 1) * count].astype(bf16)

    hid = table.shape[2]
    own_self = width // axis_count
    own_hid = hid // axis_count
    place(w_buf, 0, contract_rows(node_ref[...], pre_sum))
    place(w_buf, own_self, contract_rows(edge_ref[...], pre_buf[...]))
    place(w_buf, own_self + own_hid, contract_rows(msg_buf[...], gedge_ref[...]))
    nout = contract_rows(msg_sum, gnode_ref[...]) / nbr_count
    place(w_buf, own_self + 2 * own_hid, nout[:, :hid])
    place(w_buf, own_self + 3 * own_hid, nout[:, hid:])
    pair_copy(1, w_buf, w_mid).start()

    reduce_mid(0, s_buf, s_mid, s_own, s_in)
    reduce_mid(1, w_buf, w_mid, w_own, w_in)

    def edge_out(t, carry):
        part = pl.ds(pl.multiple_of(t * tile, tile), tile)
        dedge_ref[part, :] = (
            nt(pre_buf[part, :], wedge_ref[...]) + gedge_ref[part, :].astype(f32)
        ).astype(bf16)
        return carry

    lax.fori_loop(0, edges // tile, edge_out, 0)

    reached = reduce_end(0, s_own, s_in)
    bias_sum = jnp.sum(reached, axis=0, keepdims=True)
    reached = reached.astype(bf16)
    place(n_buf, 0, contract_rows(node_ref[...], reached))
    pair_copy(2, n_buf, n_mid).start()
    dnode_ref[...] = (
        nt(pre_sum, wself_ref[...]) + nt(reached, wnbr_ref[...]) + gnode_ref[...].astype(f32)
    ).astype(bf16)
    reduce_mid(2, n_buf, n_mid, n_own, n_in)

    count = w_in.shape[1]
    w_all[me, 0:count, :] = reduce_end(1, w_own, w_in).astype(bf16)
    high = bias_sum.astype(bf16).astype(f32)
    line = lax.broadcasted_iota(jnp.int32, (16, hid), 0)
    w_all[me, count : count + 16, :] = jnp.where(
        line == 0, high, jnp.where(line == 1, bias_sum - high, 0.0)
    ).astype(bf16)
    gather_start(1, w_all)
    n_all[me] = reduce_end(2, n_own, n_in).astype(bf16)
    gather_start(2, n_all)
    gather_forward(1, w_all)
    gather_forward(2, n_all)
    gather_finish(1, w_all)

    def unpack(out, buf, at, size, cols):
        for j in range(axis_count):
            out[j * size : (j + 1) * size, cols] = buf[j, at : at + size, :]

    unpack(dself_ref, w_all, 0, own_self, slice(0, hid))
    unpack(dein_ref, w_all, own_self, own_hid, slice(0, hid))
    unpack(deout_ref, w_all, own_self + own_hid, own_hid, slice(0, hid))
    unpack(dnout_ref, w_all, own_self + 2 * own_hid, own_hid, slice(0, hid))
    unpack(dnout_ref, w_all, own_self + 3 * own_hid, own_hid, slice(hid, 2 * hid))
    total = w_all[0, count : count + 16, :].astype(f32)
    for j in range(1, axis_count):
        total = total + w_all[j, count : count + 16, :].astype(f32)
    dbias_ref[...] = jnp.sum(total, axis=0, keepdims=True)
    gather_finish(2, n_all)
    unpack(dnbr_ref, n_all, 0, own_self, slice(0, hid))


def store_kernel(*refs):
    count = len(refs) // 2
    sems = refs[-1]
    copies = [
        pltpu.make_async_copy(refs[slot], refs[count + slot], sems.at[slot]) for slot in range(count)
    ]
    for copy in copies:
        copy.start()
    for copy in copies:
        copy.wait()


def fused(
    node_feats,
    edge_feats,
    neighbours,
    w_self,
    w_nbr,
    w_edge,
    bias,
    w_edge_out,
    w_node_out,
    grad_nodes,
    grad_edges,
):
    rows, nbr_count = neighbours.shape
    width, hid = w_self.shape
    edge_width = edge_feats.shape[2]
    edges = rows * nbr_count
    blocks = lax.axis_size("res")
    chips = blocks // 2
    nodes_all = rows * blocks
    own_w = (width + edge_width + hid + 2 * hid) // blocks
    own_n = width // blocks
    bf16, f32 = jnp.bfloat16, jnp.float32
    vmem = pl.BlockSpec(memory_space=pltpu.VMEM)
    hbm = pl.BlockSpec(memory_space=pl.ANY)

    def reduce_bufs(count):
        return [
            pltpu.VMEM((2, chips, count, hid), bf16),
            pltpu.VMEM((chips, count, hid), bf16),
            pltpu.VMEM((chips, count, hid), bf16),
            pltpu.VMEM((chips, count, hid), bf16),
        ]

    flops = 2 * edges * hid * (2 * nodes_all + 5 * edge_width)
    outs = pl.pallas_call(
        functools.partial(exchange_kernel, blocks, nbr_count),
        out_shape=(
            jax.ShapeDtypeStruct((rows, width), bf16),
            jax.ShapeDtypeStruct((edges, edge_width), bf16),
            jax.ShapeDtypeStruct((width, hid), bf16),
            jax.ShapeDtypeStruct((width, hid), bf16),
            jax.ShapeDtypeStruct((edge_width, hid), bf16),
            jax.ShapeDtypeStruct((1, hid), f32),
            jax.ShapeDtypeStruct((hid, edge_width), bf16),
            jax.ShapeDtypeStruct((hid, width), bf16),
        ),
        in_specs=[hbm, hbm, vmem, vmem, hbm, hbm, hbm, vmem, hbm, hbm, hbm, hbm],
        out_specs=[vmem] * 8,
        scratch_shapes=[
            pltpu.VMEM((rows, width), bf16),
            pltpu.VMEM((width, hid), bf16),
            pltpu.VMEM((width, hid), bf16),
            pltpu.VMEM((edge_width, hid), bf16),
            pltpu.VMEM((hid, edge_width), bf16),
            pltpu.VMEM((hid, width), bf16),
            pltpu.VMEM((rows, width), bf16),
            pltpu.VMEM((edges, edge_width), bf16),
            pltpu.VMEM((edges, edge_width), bf16),
            pltpu.SemaphoreType.DMA((9,)),
            pltpu.VMEM((blocks, rows, hid), bf16),
            pltpu.VMEM((edges, nodes_all), bf16),
            pltpu.VMEM((nodes_all, edges), bf16),
            pltpu.VMEM((edges, hid), f32),
            pltpu.VMEM((edges, hid), f32),
            pltpu.VMEM((edges, hid), bf16),
            pltpu.VMEM((edges, hid), bf16),
            pltpu.VMEM((2 * rows, hid), bf16),
            pltpu.VMEM((2 * rows, hid), bf16),
            *reduce_bufs(rows),
            *reduce_bufs(own_w),
            *reduce_bufs(own_n),
            pltpu.VMEM((blocks, own_w + 16, hid), bf16),
            pltpu.VMEM((blocks, own_n, hid), bf16),
            pltpu.SemaphoreType.DMA((3,)),
            pltpu.SemaphoreType.DMA((3,)),
            pltpu.SemaphoreType.DMA((3, chips)),
            pltpu.SemaphoreType.DMA((3, chips)),
            pltpu.SemaphoreType.DMA((3, blocks)),
            pltpu.SemaphoreType.DMA((3, blocks)),
        ],
        compiler_params=pltpu.CompilerParams(
            collective_id=0, has_side_effects=True, vmem_limit_bytes=58 * 1024 * 1024
        ),
        cost_estimate=pl.CostEstimate(flops=flops, bytes_accessed=8_000_000, transcendentals=edges * hid),
    )(
        node_feats,
        edge_feats.transpose(1, 0, 2).reshape(edges, edge_width),
        neighbours.T.reshape(edges, 1),
        neighbours.T.reshape(1, edges),
        w_self,
        w_nbr,
        w_edge,
        bias.reshape(1, hid),
        w_edge_out,
        w_node_out,
        grad_nodes,
        grad_edges.transpose(1, 0, 2).reshape(edges, edge_width),
    )
    count = len(outs)
    outs = pl.pallas_call(
        store_kernel,
        out_shape=tuple(jax.ShapeDtypeStruct(x.shape, x.dtype) for x in outs),
        in_specs=[vmem] * count,
        out_specs=[hbm] * count,
        scratch_shapes=[pltpu.SemaphoreType.DMA((count,))],
        compiler_params=pltpu.CompilerParams(vmem_limit_bytes=58 * 1024 * 1024),
    )(*outs)
    d_nodes, d_edges, d_self, d_nbr, d_ein, d_bias, d_eout, d_nout = outs
    return (
        d_nodes,
        d_edges.reshape(nbr_count, rows, edge_width).transpose(1, 0, 2),
        d_self,
        d_nbr,
        d_ein,
        d_bias.reshape(hid),
        d_eout,
        d_nout,
    )


def local(
    node_feats,
    edge_feats,
    neighbours,
    w_self,
    w_nbr,
    w_edge,
    bias,
    w_edge_out,
    w_node_out,
    grad_nodes,
    grad_edges,
):
    res_rows = node_feats.shape[0]
    nbr_count = neighbours.shape[1]
    node_width = node_feats.shape[1]
    edge_width = edge_feats.shape[2]
    hidden = w_self.shape[1]
    edges_dev = res_rows * nbr_count
    blocks_res = lax.axis_size("res")
    nodes_all = res_rows * blocks_res
    edge_flat = edge_feats.reshape(edges_dev, edge_width)
    gedge_flat = grad_edges.reshape(edges_dev, edge_width)
    projected = jnp.dot(node_feats, w_nbr, preferred_element_type=jnp.float32).astype(jnp.bfloat16)
    table = lax.all_gather(projected, "res", axis=0, tiled=True)
    picks = (
        neighbours.reshape(-1)[:, None] == jnp.arange(nodes_all, dtype=jnp.int32)[None, :]
    ).astype(jnp.bfloat16)
    preact = (jnp.dot(node_feats, w_self, preferred_element_type=jnp.float32) + bias)[:, None, :]
    preact = preact + (
        jnp.dot(edge_flat, w_edge, preferred_element_type=jnp.float32)
        + jnp.dot(picks, table, preferred_element_type=jnp.float32)
    ).reshape(res_rows, nbr_count, hidden)
    values, slopes = gelu_parts(preact)
    message = values.astype(jnp.bfloat16)
    grad_msg = jnp.dot(gedge_flat, w_edge_out.T, preferred_element_type=jnp.float32).reshape(
        res_rows, nbr_count, hidden
    )
    grad_msg = (
        grad_msg
        + (jnp.dot(grad_nodes, w_node_out.T, preferred_element_type=jnp.float32) / nbr_count)[
            :, None, :
        ]
    )
    grad_pre = (grad_msg * slopes).astype(jnp.bfloat16)
    pre_flat = grad_pre.reshape(edges_dev, hidden)
    msg_flat = message.reshape(edges_dev, hidden)
    pre_sum = jnp.sum(grad_pre.astype(jnp.float32), axis=1).astype(jnp.bfloat16)
    msg_sum = jnp.sum(message.astype(jnp.float32), axis=1).astype(jnp.bfloat16)
    spread = contract_rows(picks, pre_flat).astype(jnp.bfloat16)
    landed = lax.all_to_all(
        spread.reshape(blocks_res, res_rows, hidden), "res", split_axis=0, concat_axis=0, tiled=True
    )
    reached = jnp.sum(landed.astype(jnp.float32), axis=0).astype(jnp.bfloat16)
    terms = (
        contract_rows(node_feats, pre_sum),
        contract_rows(node_feats, reached),
        contract_rows(edge_flat, pre_flat),
        contract_rows(msg_flat, gedge_flat),
        contract_rows(msg_sum, grad_nodes) / nbr_count,
    )
    packed = jnp.concatenate(
        [t.astype(jnp.bfloat16).reshape(blocks_res, -1, 128) for t in terms], axis=1
    )
    swapped = lax.all_to_all(packed, "res", split_axis=0, concat_axis=0, tiled=True)
    mine = jnp.sum(swapped.astype(jnp.float32), axis=0).astype(jnp.bfloat16)
    totals = lax.all_gather(mine, "res", axis=0, tiled=False)
    outs = []
    start = 0
    for t in terms:
        rows = t.size // blocks_res // 128
        outs.append(totals[:, start : start + rows].reshape(t.shape))
        start += rows
    grad_self, grad_nbr, grad_edge_in, grad_eout, grad_nout = outs
    grad_bias = lax.psum(jnp.sum(pre_flat.astype(jnp.float32), axis=0), "res")
    feat_index = lax.axis_index("feat")
    feat_count = lax.axis_size("feat")
    edge_part = edge_width // feat_count
    node_part = node_width // feat_count
    full_pre, full_wedge = (
        lax.all_gather(pre_flat, "feat", axis=1, tiled=True),
        lax.all_gather(w_edge, "feat", axis=1, tiled=True),
    )
    own_wedge = lax.dynamic_slice_in_dim(full_wedge, feat_index * edge_part, edge_part, 0)
    edge_summed = jnp.dot(full_pre, own_wedge.T, preferred_element_type=jnp.float32)
    gedge_part = lax.dynamic_slice_in_dim(gedge_flat, feat_index * edge_part, edge_part, 1).astype(
        jnp.float32
    )
    d_edges = (
        (edge_summed + gedge_part).astype(jnp.bfloat16).reshape(res_rows, nbr_count, edge_part)
    )
    node_total = jnp.dot(pre_sum, w_self.T, preferred_element_type=jnp.float32) + jnp.dot(
        reached, w_nbr.T, preferred_element_type=jnp.float32
    )
    node_total = lax.psum_scatter(node_total, "feat", scatter_dimension=1, tiled=True)
    gnode_part = lax.dynamic_slice_in_dim(grad_nodes, feat_index * node_part, node_part, 1).astype(
        jnp.float32
    )
    d_nodes = (node_total + gnode_part).astype(jnp.bfloat16)
    return (d_nodes, d_edges, grad_self, grad_nbr, grad_edge_in, grad_bias, grad_eout, grad_nout)


def solution(mesh):
    in_specs = (
        P(("groups", "res"), None),
        P(("groups", "res"), None, None),
        P(("groups", "res"), None),
        P(None, "feat"),
        P(None, "feat"),
        P(None, "feat"),
        P("feat"),
        P("feat", None),
        P("feat", None),
        P(("groups", "res"), None),
        P(("groups", "res"), None, None),
    )
    out_specs = (
        P(("groups", "res"), "feat"),
        P(("groups", "res"), None, "feat"),
        P("groups", "feat"),
        P("groups", "feat"),
        P("groups", "feat"),
        P(("groups", "feat")),
        P(("groups", "feat"), None),
        P(("groups", "feat"), None),
    )
    short = mesh.shape["res"] == 16 and mesh.shape["feat"] == 1
    body = fused if short else local
    return jax.shard_map(body, mesh=mesh, in_specs=in_specs, out_specs=out_specs, check_vma=False)
```
